32 devices in a mesh: tp: 8 (over y, x, core), grp: 4 (over z).
Axes of the slice: x: 2, y: 2, z: 4, core: 2. Of those that a mesh axis runs over, the one named last changes fastest.
Arguments:
- resid_in: bfloat16 [256, 8192], P('grp', 'tp'), may hold values from -6 to 6
- queries: bfloat16 [256, 4096], P('grp', 'tp')
- kv_cache: bfloat16 [2, 256, 8, 128, 128], P(None, 'grp', 'tp'), as said below
- new_kv: bfloat16 [2, 256, 4, 128], P(None, 'grp')
- lengths: int32 [256], P('grp'), may hold values from 1 to 128, 16384 in all
- out_weight: bfloat16 [4096, 8192], P('tp'), may hold values from -0.09375 to 0.09375
- enc_weight: bfloat16 [8192, 32768], P('tp', 'grp'), may hold values from -0.0625 to 0.0625
- enc_bias: float32 [32768], P('grp'), may hold values from -1 to 0.5
- dec_weight: bfloat16 [32768, 8192], P('grp', 'tp'), may hold values from -0.75 to 0.75
- clamp_ids: int32 [256, 4], P('grp'), may hold values from 0 to 32767, as said below
- clamp_values: float32 [256, 4], P('grp'), may hold values from 2 to 8
Outputs:
- resid_out: bfloat16 [256, 8192], P('grp', 'tp')
- features: bfloat16 [256, 32768], P('tp', 'grp')
The draws below stay inside these ranges and needn't reach their ends.
Inputs may be any that keep to these rules, and one draw needn't show every extreme that they name: Entries of kv_cache whose third index divided by 2 agrees are equal. `clamp_ids`: a row's 4 ids are (b + c * 8192) modulo 32768 for c = 0 .. 3.
All inputs are finite; a program needn't handle non-finite values. No bound on the sum of `lengths` on one device may be relied on, other than what follows from the above.
Results may differ from the reference program's by a relative error of at most 0.008.
Values may be sent and summed in bfloat16 or wider, within the bound.
A program may use at most 128 MiB of HBM per device.

```python
import math
import jax
import jax.numpy as jnp
import numpy as np
from jax import lax

D = 8192
HEAD_DIM = 128
HEADS = 32
KV_HEADS = 4
LATENTS = 32768
CLAMPS = 4
CACHE_LEN = 128
SEQS = 256
KV_COPIES = 8


def draw_queries(key, part):
    group_size = HEADS // KV_HEADS
    shape = (SEQS, KV_HEADS, group_size, HEAD_DIM)
    base = jnp.clip(jax.random.normal(jax.random.fold_in(key, 11), shape, jnp.float32), -6.0, 6.0)
    return base.reshape(SEQS, HEADS * HEAD_DIM).astype(jnp.bfloat16)


def draw_kv_cache(key, part):
    shape = (2, SEQS, KV_HEADS, CACHE_LEN, HEAD_DIM)
    base = jnp.clip(jax.random.normal(jax.random.fold_in(key, 12), shape, jnp.float32), -6.0, 6.0)
    return jnp.repeat(base, KV_COPIES // KV_HEADS, axis=2).astype(jnp.bfloat16)


def draw_new_kv(key, part):
    shape = (2, SEQS, KV_HEADS, HEAD_DIM)
    base = jnp.clip(jax.random.normal(jax.random.fold_in(key, 13), shape, jnp.float32), -6.0, 6.0)
    return base.astype(jnp.bfloat16)


def draw_clamp_ids(key, part):
    first_id = jax.random.randint(jax.random.fold_in(key, 5), (SEQS, 1), 0, LATENTS, dtype=jnp.int32)
    row_index = jnp.arange(SEQS, dtype=jnp.int32)[:, None]
    first_id = jnp.where(row_index == 0, LATENTS - 1, first_id)
    first_id = jnp.where(row_index == 1, 0, first_id)
    spacing = jnp.arange(CLAMPS, dtype=jnp.int32)[None, :] * (LATENTS // CLAMPS)
    return ((first_id + spacing) % LATENTS).astype(jnp.int32)


def levels(rng, extent, split, least, high):
    gain = 1.0
    for position, blocks in split:
        steps = jax.random.uniform(jax.random.fold_in(jax.random.fold_in(rng, 6), position), (blocks,), jnp.float32, least / len(split), high / len(split))
        gain = gain * jnp.repeat(jnp.exp(steps), extent[position] // blocks).reshape((-1,) + (1,) * (len(extent) - 1 - position))
    return gain


def split_up(number_of, total, reach, lean):
    weights = [(1 << 20) // math.isqrt(grade ** lean) + 1 for grade in range(2, number_of + 1)]
    spare, given = total - reach - (number_of - 1), [1] * (number_of - 1)
    while spare > 0:
        movable = [i for i in range(number_of - 1) if given[i] < reach]
        pool, left = sum([weights[i] for i in movable]), spare
        for i in movable:
            more = min(reach - given[i], max(1, left * weights[i] // pool), spare)
            given[i] = given[i] + more
            spare = spare - more
    return np.array([reach] + given)


def ragged_sizes(key, number_of, total, most, slope):
    if number_of == 2:
        one = jax.random.randint(key, (), max(1, total - most), min(most, total - 1) + 1)
        return jnp.stack([one, total - one])
    sizes = jnp.asarray(split_up(number_of, total, most, slope), jnp.int32)
    couples = (number_of - 1) // 2
    donor, taker = sizes[1:1 + 2 * couples:2], sizes[2:2 + 2 * couples:2]
    margin = jnp.minimum(donor - 1, most - taker)
    shifted = jax.random.randint(jax.random.fold_in(key, 1), (couples,), 0, 1 << 20) % (margin + 1)
    sizes = sizes.at[1:1 + 2 * couples:2].set(donor - shifted).at[2:2 + 2 * couples:2].set(taker + shifted)
    return sizes[jax.random.permutation(jax.random.fold_in(key, 2), number_of)]


def centred(key, extent, spread, bound, pieces=(), kind=jnp.bfloat16):
    values = spread * jax.random.normal(key, extent, jnp.float32)
    if pieces:
        values = values * levels(key, extent, pieces, -0.22, 0.18)
    return jnp.clip(values, -bound, bound).astype(kind)


def setup_inputs(seed: int = 0) -> dict:
    arg_keys = jax.random.split(jax.random.key(seed), 12)
    return {
        "resid_in": centred(arg_keys[0], (SEQS, D), 1.0, 6.0, ((0, 4), (1, 8))),
        "queries": draw_queries(jax.random.fold_in(arg_keys[11], 71), 0),
        "kv_cache": draw_kv_cache(jax.random.fold_in(arg_keys[11], 71), 0),
        "new_kv": draw_new_kv(jax.random.fold_in(arg_keys[11], 71), 0),
        "lengths": ragged_sizes(arg_keys[4], SEQS, SEQS * CACHE_LEN // 2, CACHE_LEN, 2).astype(jnp.int32),
        "out_weight": centred(arg_keys[5], (HEADS * HEAD_DIM, D), (HEADS * HEAD_DIM) ** -0.5, 0.09375, ((0, 8),)),
        "enc_weight": centred(arg_keys[6], (D, LATENTS), D ** -0.5, 0.0625, ((0, 8), (1, 4))),
        "enc_bias": jnp.clip(-1.0 + 1.5 * jax.random.uniform(arg_keys[7], (LATENTS,), jnp.float32) ** levels(arg_keys[7], (LATENTS,), ((0, 4),), -0.2, 0.2), -1.0, 0.5),
        "dec_weight": centred(arg_keys[8], (LATENTS, D), 64 ** -0.5, 0.75, ((0, 4), (1, 8))),
        "clamp_ids": draw_clamp_ids(jax.random.fold_in(arg_keys[11], 71), 0),
        "clamp_values": jnp.clip(2.0 + 6.0 * jax.random.uniform(arg_keys[10], (SEQS, CLAMPS), jnp.float32) ** levels(arg_keys[10], (SEQS, CLAMPS), ((0, 4),), -0.2, 0.2), 2.0, 8.0),
    }


def reference(resid_in, queries, kv_cache, new_kv, lengths, out_weight, enc_weight, enc_bias, dec_weight, clamp_ids, clamp_values):
    group_size = HEADS // KV_HEADS
    score_scale = HEAD_DIM ** -0.5
    cache_view = kv_cache[:, :, ::(KV_COPIES // KV_HEADS)]
    query_heads = queries.astype(jnp.float32).reshape(SEQS, KV_HEADS, group_size, HEAD_DIM)
    cache_keys = cache_view[0].astype(jnp.float32)
    cache_values = cache_view[1].astype(jnp.float32)
    scores = jnp.einsum("skgd,skpd->skgp", query_heads, cache_keys) * score_scale
    new_score = jnp.einsum("skgd,skd->skg", query_heads, new_kv[0].astype(jnp.float32)) * score_scale
    slot_index = jnp.arange(CACHE_LEN, dtype=jnp.int32)
    is_valid = (slot_index[None, :] < lengths[:, None])[:, None, None, :]
    top_score = jnp.maximum(jnp.max(jnp.where(is_valid, scores, -jnp.inf), axis=-1), new_score)
    prob_cache = jnp.where(is_valid, jnp.exp(scores - top_score[..., None]), 0.0)
    new_prob = jnp.exp(new_score - top_score)
    total_weight = jnp.sum(prob_cache, axis=-1) + new_prob
    cache_rounded = lax.optimization_barrier(prob_cache.astype(jnp.bfloat16)).astype(jnp.float32)
    new_rounded = lax.optimization_barrier(new_prob.astype(jnp.bfloat16)).astype(jnp.float32)
    weighted = jnp.einsum("skgp,skpd->skgd", cache_rounded, cache_values)
    weighted = weighted + new_rounded[..., None] * new_kv[1].astype(jnp.float32)[:, :, None, :]
    head_output = (weighted / total_weight[..., None]).astype(jnp.bfloat16).reshape(SEQS, HEADS * HEAD_DIM)
    attn_out = jnp.dot(head_output, out_weight, preferred_element_type=jnp.float32)
    resid_mid = (resid_in.astype(jnp.float32) + attn_out).astype(jnp.bfloat16)
    pre_act = jnp.dot(resid_mid.astype(jnp.float32), enc_weight.astype(jnp.float32))
    features = jnp.maximum(pre_act + enc_bias, 0.0).astype(jnp.bfloat16)
    clamped_now = jnp.take_along_axis(features, clamp_ids, axis=1).astype(jnp.float32)
    delta_at = (clamp_values - clamped_now).astype(jnp.bfloat16)
    decoder_rows = dec_weight[clamp_ids]
    edit_sum = jnp.einsum("sc,scd->sd", delta_at.astype(jnp.float32), decoder_rows.astype(jnp.float32))
    resid_out = (resid_mid.astype(jnp.float32) + edit_sum).astype(jnp.bfloat16)
    return resid_out, features
```

```python
import jax
import jax.numpy as jnp
from jax import lax
from jax.sharding import PartitionSpec as P

HEAD_DIM = 128
KV_HEADS = 4


def per_device(
    resid_in,
    queries,
    kv_cache,
    new_kv,
    lengths,
    out_weight,
    enc_weight,
    enc_bias,
    dec_weight,
    clamp_ids,
    clamp_values,
):
    tp_count = lax.axis_size("tp")
    tp_rank = lax.axis_index("tp")
    grp_rank = lax.axis_index("grp")
    row_count = resid_in.shape[0]
    own_heads = queries.shape[1] // HEAD_DIM
    slot_count = kv_cache.shape[3]
    score_scale = HEAD_DIM ** (-0.5)
    query_heads = queries.reshape(row_count, own_heads, HEAD_DIM)
    cache_keys = kv_cache[0, :, 0]
    cache_values = kv_cache[1, :, 0]
    kv_index = tp_rank // (tp_count // KV_HEADS)
    new_key = lax.dynamic_index_in_dim(new_kv[0], kv_index, 1, keepdims=False)
    new_value = lax.dynamic_index_in_dim(new_kv[1], kv_index, 1, keepdims=False)
    scores = (
        jnp.einsum("shd,spd->shp", query_heads, cache_keys, preferred_element_type=jnp.float32)
        * score_scale
    )
    new_score = (
        jnp.einsum("shd,sd->sh", query_heads, new_key, preferred_element_type=jnp.float32)
        * score_scale
    )
    slot_index = jnp.arange(slot_count, dtype=jnp.int32)
    is_valid = (slot_index[None, :] < lengths[:, None])[:, None, :]
    top_score = jnp.maximum(jnp.max(jnp.where(is_valid, scores, -jnp.inf), axis=-1), new_score)
    prob_cache = jnp.where(is_valid, jnp.exp(scores - top_score[..., None]), 0.0)
    new_prob = jnp.exp(new_score - top_score)
    total_weight = jnp.sum(prob_cache, axis=-1) + new_prob
    new_rounded = lax.optimization_barrier(new_prob.astype(jnp.bfloat16)).astype(jnp.float32)
    weighted = jnp.einsum(
        "shp,spd->shd",
        prob_cache.astype(jnp.bfloat16),
        cache_values,
        preferred_element_type=jnp.float32,
    )
    weighted = weighted + new_rounded[..., None] * new_value.astype(jnp.float32)[:, None, :]
    head_output = (
        (weighted / total_weight[..., None])
        .astype(jnp.bfloat16)
        .reshape(row_count, own_heads * HEAD_DIM)
    )
    attn_part = jnp.dot(head_output, out_weight, preferred_element_type=jnp.float32)
    attn_cols = lax.psum_scatter(
        attn_part.astype(jnp.bfloat16), "tp", scatter_dimension=1, tiled=True
    ).astype(jnp.float32)
    resid_mid = (resid_in.astype(jnp.float32) + attn_cols).astype(jnp.bfloat16)
    table = lax.all_gather(
        jnp.concatenate([clamp_ids.astype(jnp.float32), clamp_values], axis=1),
        "grp", axis=0, tiled=True,
    )
    slots = clamp_ids.shape[1]
    lat_span = enc_weight.shape[1]
    local = table[:, :slots].astype(jnp.int32) - grp_rank * lat_span
    inside = (local >= 0) & (local < lat_span)
    hit_any = jnp.any(inside, axis=1)
    local_id = jnp.sum(jnp.where(inside, local, 0), axis=1)
    target = jnp.sum(jnp.where(inside, table[:, slots:], 0.0), axis=1)
    pre_part = jnp.dot(
        lax.all_gather(resid_mid, "grp", axis=0, tiled=True),
        enc_weight,
        preferred_element_type=jnp.float32,
    )
    columns = jnp.arange(lat_span, dtype=jnp.int32)
    is_hit = columns[None, :] == local_id[:, None]
    picked = lax.psum(jnp.sum(jnp.where(is_hit, pre_part, 0.0), axis=1), "tp")
    pre_act = lax.psum_scatter(
        pre_part.astype(jnp.bfloat16), "tp", scatter_dimension=0, tiled=True
    ).astype(jnp.float32)
    feature_out = jnp.maximum(pre_act + enc_bias, 0.0).astype(jnp.bfloat16)
    current = jnp.maximum(picked + enc_bias[local_id], 0.0).astype(jnp.bfloat16)
    delta = (target - current.astype(jnp.float32)).astype(jnp.bfloat16).astype(jnp.float32)
    delta = jnp.where(hit_any, delta, 0.0)
    edit_part = delta[:, None] * dec_weight[local_id].astype(jnp.float32)
    edit_mine = lax.psum_scatter(
        edit_part.astype(jnp.bfloat16), "grp", scatter_dimension=0, tiled=True
    ).astype(jnp.float32)
    resid_out = (resid_mid.astype(jnp.float32) + edit_mine).astype(jnp.bfloat16)
    return (resid_out, feature_out)


def solution(mesh):
    placed = (
        P("grp", "tp"),
        P("grp", "tp"),
        P(None, "grp", "tp", None, None),
        P(None, "grp", None, None),
        P("grp"),
        P("tp", None),
        P("tp", "grp"),
        P("grp"),
        P("grp", "tp"),
        P("grp", None),
        P("grp", None),
    )
    return jax.shard_map(
        per_device,
        mesh=mesh,
        in_specs=placed,
        out_specs=(P("grp", "tp"), P("tp", "grp")),
        check_vma=False,
    )
```

```python
import functools

import jax
import jax.numpy as jnp
from jax import lax
from jax.experimental import pallas as pl
from jax.experimental.pallas import tpu as pltpu
from jax.sharding import PartitionSpec as P

HEAD_DIM = 128
KV_HEADS = 4
CHUNKS = 2
PARTS = 4
DEC_BLOCKS = 8
DEC_SLOTS = 4
TILE = 256
MESH = pl.DeviceIdType.MESH


def bits_of(count):
    found, bit = [], 1
    while bit < count:
        found.append(bit)
        bit *= 2
    return found


def flip(rank, pattern, count):
    for bit in bits_of(count):
        if pattern & bit:
            rank = rank + bit * (1 - 2 * lax.rem(lax.div(rank, bit), 2))
    return rank


def stage_plan(count, ascending):
    order = bits_of(count)
    order = order if ascending else order[:1] + order[:0:-1]
    held, stages = list(range(count)), []
    for bit in order:
        keep = [i for i, e in enumerate(held) if not e & bit]
        send = [held.index(held[i] + bit) for i in keep]
        stages.append((bit, keep, send))
        held = [held[i] for i in keep]
    return stages


def layer_kernel(
    cfg,
    ho_ref, resid_ref, table_ref, bias_ref, outw_ref, enc_ref, dec_ref,
    resid_out_ref, feat_ref,
    ho_p, outw_v, enc_v, dec_v,
    a_keep, a_send, a_recv,
    xg, xp, tg, lid_d, lid_e,
    p_keep, p_send, p_recv,
    acc, picked, pk_send, pk_recv, rows, delta, e_send, e_recv,
    outw_sem, enc_sem, dec_sem,
    a_ss, a_rs, x_ss, x_rs, t_ss, t_rs, p_ss, p_rs, k_ss, k_rs, e_ss, e_rs,
):
    tp_n, g_n, slots = cfg
    t, g = lax.axis_index("tp"), lax.axis_index("grp")
    q, _, h, width = resid_ref.shape
    lat = bias_ref.shape[1]
    span = lat // PARTS
    half = q * h
    rows_m = tp_n * h
    block = lat // DEC_BLOCKS
    own = pl.ds(g * q, q)
    tile = min(TILE, span)

    def remote(src, dst, ss, rs, axis, other):
        return pltpu.make_async_remote_copy(
            src_ref=src, dst_ref=dst, send_sem=ss, recv_sem=rs,
            device_id={axis: other}, device_id_type=MESH,
        )

    order_e = [e for e in range(tp_n) if e & 1] + [e for e in range(tp_n) if not e & 1]

    def outw_copy(e):
        cols = pl.ds(pl.multiple_of(flip(t, e, tp_n) * width, width), width)
        return pltpu.make_async_copy(outw_ref.at[:, cols], outw_v.at[e], outw_sem.at[e])

    def enc_copy(c):
        return pltpu.make_async_copy(
            enc_ref.at[:, pl.ds(c * span, span)], enc_v.at[c], enc_sem.at[c]
        )

    def dec_copy(b):
        return pltpu.make_async_copy(
            dec_ref.at[pl.ds(b * block, block)], dec_v.at[b % DEC_SLOTS], dec_sem.at[b]
        )

    for e in order_e:
        outw_copy(e).start()

    barrier = pltpu.get_barrier_semaphore()
    for e in range(1, tp_n):
        pl.semaphore_signal(
            barrier, inc=1, device_id={"tp": flip(t, e, tp_n)}, device_id_type=MESH
        )
    for e in range(1, g_n):
        pl.semaphore_signal(
            barrier, inc=1, device_id={"grp": flip(g, e, g_n)}, device_id_type=MESH
        )
    for j in range(CHUNKS):
        ho_p[j] = ho_ref[:, j].reshape(half, ho_ref.shape[3])
    tg[own] = table_ref[...]
    pl.semaphore_wait(barrier, tp_n + g_n - 2)

    table_copies = []
    for e in range(1, g_n):
        copy = remote(
            table_ref, tg.at[own], t_ss.at[e], t_rs.at[e], "grp", flip(g, e, g_n)
        )
        copy.start()
        table_copies.append(copy)

    plans = [stage_plan(tp_n, True), stage_plan(tp_n, False)]
    n_stage = len(plans[0])

    def a_copy(j, k):
        bit = plans[j % 2][k][0]
        count = tp_n >> (k + 1)
        first = tp_n - 2 * count
        part = pl.ds(first, count)
        return remote(
            a_send.at[j, part], a_recv.at[j, part], a_ss.at[j, k], a_rs.at[j, k],
            "tp", flip(t, bit, tp_n),
        )

    for place, e in enumerate(order_e):
        outw_copy(e).wait()
        part = jnp.dot(
            ho_p[...].reshape(CHUNKS * half, ho_p.shape[2]), outw_v[e],
            preferred_element_type=jnp.float32,
        )
        for j in range(CHUNKS):
            mine = part[j * half : (j + 1) * half]
            if e & 1:
                a_send[j, e >> 1] = mine.astype(jnp.bfloat16)
            else:
                a_keep[j, e >> 1] = mine
        if place == tp_n // 2 - 1:
            for j in range(CHUNKS):
                a_copy(j, 0).start()
    for c in range(PARTS):
        enc_copy(c).start()
    for b in range(DEC_SLOTS):
        dec_copy(b).start()

    def held_at(plan, k):
        held = list(range(tp_n // 2))
        for _, stay, _ in plan[1 : k + 1]:
            held = [held[s] for s in stay]
        return held

    def fold(keep, send, recv, copy, plan, j, k):
        copy(j, k - 1).wait()
        count = tp_n >> k
        first = tp_n - 2 * count
        held = held_at(plan, k - 1)
        for i, slot in enumerate(held):
            keep[j, slot] = keep[j, slot] + recv[j, first + i].astype(jnp.float32)
        if k < n_stage:
            go = plan[k][2]
            nxt = tp_n - 2 * (count // 2)
            for i, s in enumerate(go):
                send[j, nxt + i] = keep[j, held[s]].astype(jnp.bfloat16)
            copy(j, k).start()

    for k in range(1, n_stage + 1):
        for j in range(CHUNKS):
            fold(a_keep, a_send, a_recv, a_copy, plans[j % 2], j, k)

    x_copies = [[], []]
    for j in range(CHUNKS):
        mid = resid_ref[:, j].astype(jnp.float32) + a_keep[j, 0].reshape(q, h, width)
        xg[j, own] = mid.astype(jnp.bfloat16)
        for e in range(1, g_n):
            copy = remote(
                xg.at[j, own], xg.at[j, own], x_ss.at[j, e], x_rs.at[j, e],
                "grp", flip(g, e, g_n),
            )
            copy.start()
            x_copies[j].append(copy)

    for copy in table_copies:
        copy.wait()
    low = (g * lat).astype(jnp.float32)
    for j in range(CHUNKS):
        found = tg[:, j].reshape(rows_m, 128)
        local = jnp.full((rows_m, 1), -1.0, jnp.float32)
        value = jnp.zeros((rows_m, 1), jnp.float32)
        for c in range(slots):
            place = found[:, c : c + 1] - low
            inside = (place >= 0.0) & (place < float(lat))
            local = jnp.where(inside, place, local)
            value = jnp.where(inside, found[:, slots + c : slots + c + 1], value)
        wide = jnp.broadcast_to(local, (rows_m, 128)).astype(jnp.int32)
        lid_d[j] = wide.reshape(tp_n, h, 128)
        delta[j] = jnp.broadcast_to(value, (rows_m, 128)).reshape(tp_n, h, 128)
    for j in range(CHUNKS):
        for e in range(tp_n):
            lid_e[j, e] = lid_d[j, flip(t, e, tp_n)]
    acc[...] = jnp.zeros_like(acc)
    rows[...] = jnp.zeros_like(rows)

    def dec_step(b):
        dec_copy(b).wait()
        lane = lax.broadcasted_iota(jnp.int32, (CHUNKS * rows_m, 128), 1)
        local = lid_d[...].reshape(CHUNKS * rows_m, 128)
        pieces = [
            jnp.where(local == lane + (b * block + n), 1.0, 0.0).astype(jnp.bfloat16)
            for n in range(0, block, 128)
        ]
        hot = jnp.concatenate(pieces, axis=1)
        got = jnp.dot(hot, dec_v[b % DEC_SLOTS], preferred_element_type=jnp.float32)
        rows[...] += got.reshape(rows.shape)
        if b + DEC_SLOTS < DEC_BLOCKS:
            dec_copy(b + DEC_SLOTS).start()

    for b in range(DEC_SLOTS):
        dec_step(b)

    pieces = CHUNKS * PARTS
    bias_on = jnp.where(t == 0, 1.0, 0.0).astype(jnp.float32)

    def p_copy(p, k):
        bit = plans[p % 2][k][0]
        count = tp_n >> (k + 1)
        part = pl.ds(tp_n - 2 * count, count)
        return remote(
            p_send.at[p, part], p_recv.at[p, part], p_ss.at[p, k], p_rs.at[p, k],
            "tp", flip(t, bit, tp_n),
        )

    def multiply(p):
        j, c = p // PARTS, p % PARTS
        if c == 0:
            for copy in x_copies[j]:
                copy.wait()
            for e in range(tp_n):
                xp[j, e] = xg[j, flip(t, e, tp_n)]
        if j == 0:
            enc_copy(c).wait()

        def body(n, _):
            cols = pl.ds(pl.multiple_of(n * tile, tile), tile)
            part = jnp.dot(
                xp[j].reshape(rows_m, width), enc_v[c, :, cols],
                preferred_element_type=jnp.float32,
            )
            lane = lax.broadcasted_iota(jnp.int32, (rows_m, 128), 1)
            local = lid_e[j].reshape(rows_m, 128)
            total = acc[j].reshape(rows_m, 128)
            for m in range(0, tile, 128):
                at = pl.multiple_of(c * span + n * tile + m, 128)
                shift = bias_ref[:, pl.ds(at, 128)] * bias_on
                total = total + jnp.where(
                    local == lane + at, part[:, m : m + 128] + shift, 0.0
                )
            acc[j] = total.reshape(tp_n, h, 128)
            for e in range(tp_n):
                rows_e = part[e * h : (e + 1) * h]
                if e & 1:
                    p_send[p, e >> 1, :, cols] = rows_e.astype(jnp.bfloat16)
                else:
                    p_keep[p, e >> 1, :, cols] = rows_e
            return 0

        lax.fori_loop(0, span // tile, body, 0)
        p_copy(p, 0).start()

    def finish(p):
        j, c = p // PARTS, p % PARTS
        cols = pl.ds(c * span, span)
        whole = p_keep[p, 0] + bias_ref[:, cols]
        feat_ref[pl.ds(j * h, h), cols] = jnp.maximum(whole, 0.0).astype(jnp.bfloat16)

    eye = lax.broadcasted_iota(jnp.int32, (rows_m, rows_m), 0) == lax.broadcasted_iota(
        jnp.int32, (rows_m, rows_m), 1
    )

    def pick_copy(j, e):
        return remote(
            pk_send.at[j], pk_recv.at[j, e], k_ss.at[j, e], k_rs.at[j, e],
            "tp", flip(t, e, tp_n),
        )

    def pick(j):
        for e in range(tp_n):
            picked[j, flip(t, e, tp_n)] = acc[j, e]
        column = jnp.sum(picked[j].reshape(rows_m, 128), axis=1, keepdims=True)
        line = jnp.sum(jnp.where(eye, column, 0.0), axis=0, keepdims=True)
        pk_send[j] = jnp.broadcast_to(line, (8, rows_m))
        for e in range(1, tp_n):
            pick_copy(j, e).start()

    def edit_copy(j, e):
        return remote(
            e_send.at[j, e], e_recv.at[j, e], e_ss.at[j, e], e_rs.at[j, e],
            "grp", flip(g, e, g_n),
        )

    def edit(j):
        line = pk_send[j]
        for e in range(1, tp_n):
            pick_copy(j, e).wait()
            line = line + pk_recv[j, e]
        column = jnp.sum(jnp.where(eye, line[:1], 0.0), axis=1, keepdims=True)
        now = jnp.maximum(column, 0.0).astype(jnp.bfloat16).astype(jnp.float32)
        change = delta[j].reshape(rows_m, 128)[:, :1] - now
        change = change.astype(jnp.bfloat16).astype(jnp.float32)
        delta[j] = jnp.broadcast_to(change, (rows_m, 128)).reshape(tp_n, h, 128)
        for e in range(1, g_n):
            there = pl.ds(flip(g, e, g_n) * q, q)
            step = delta[j, there]
            e_send[j, e] = (rows[j, there] * step[:, :, :1]).astype(jnp.bfloat16)
            edit_copy(j, e).start()

    def close(j):
        total = xg[j, own].astype(jnp.float32)
        edits = rows[j, own] * delta[j, own][:, :, :1]
        for e in range(1, g_n):
            edit_copy(j, e).wait()
            edits = edits + e_recv[j, e].astype(jnp.float32)
        resid_out_ref[:, j] = (total + edits).astype(jnp.bfloat16)

    for s in range(pieces + n_stage):
        if s < pieces:
            multiply(s)
            if s % PARTS == PARTS - 1:
                pick(s // PARTS)
        for k in range(n_stage, 0, -1):
            p = s - k
            if 0 <= p < pieces:
                fold(p_keep, p_send, p_recv, p_copy, plans[p % 2], p, k)
                if k == n_stage:
                    finish(p)
        if s < DEC_BLOCKS - DEC_SLOTS:
            dec_step(s + DEC_SLOTS)
        if s == PARTS:
            edit(0)
        if s == pieces:
            edit(1)
    for j in range(CHUNKS):
        close(j)


def layer(ho, resid_in, table, enc_bias, out_weight, enc_weight, dec_weight, slots):
    tp_n, g_n = lax.axis_size("tp"), lax.axis_size("grp")
    rc, width = resid_in.shape
    depth = ho.shape[1]
    lat = enc_weight.shape[1]
    out_rows = rc * g_n // tp_n
    q, h = rc // out_rows, out_rows // CHUNKS
    half = q * h
    span, block = lat // PARTS, lat // DEC_BLOCKS
    pieces = CHUNKS * PARTS
    n_stage = len(bits_of(tp_n))
    bf16, f32 = jnp.bfloat16, jnp.float32
    vmem = pl.BlockSpec(memory_space=pltpu.VMEM)
    hbm = pl.BlockSpec(memory_space=pl.ANY)
    dma = pltpu.SemaphoreType.DMA
    resid_out, feat = pl.pallas_call(
        functools.partial(layer_kernel, (tp_n, g_n, slots)),
        out_shape=(
            jax.ShapeDtypeStruct((q, CHUNKS, h, width), bf16),
            jax.ShapeDtypeStruct((out_rows, lat), bf16),
        ),
        in_specs=[vmem, vmem, vmem, vmem, hbm, hbm, hbm],
        out_specs=(vmem, vmem),
        scratch_shapes=[
            pltpu.VMEM((CHUNKS, half, depth), bf16),
            pltpu.VMEM((tp_n, depth, width), bf16),
            pltpu.VMEM((PARTS, width, span), bf16),
            pltpu.VMEM((DEC_SLOTS, block, width), bf16),
            pltpu.VMEM((CHUNKS, tp_n // 2, half, width), f32),
            pltpu.VMEM((CHUNKS, tp_n - 1, half, width), bf16),
            pltpu.VMEM((CHUNKS, tp_n - 1, half, width), bf16),
            pltpu.VMEM((CHUNKS, tp_n, h, width), bf16),
            pltpu.VMEM((CHUNKS, tp_n, h, width), bf16),
            pltpu.VMEM((tp_n, CHUNKS, h, 128), f32),
            pltpu.VMEM((CHUNKS, tp_n, h, 128), jnp.int32),
            pltpu.VMEM((CHUNKS, tp_n, h, 128), jnp.int32),
            pltpu.VMEM((pieces, tp_n // 2, h, span), f32),
            pltpu.VMEM((pieces, tp_n - 1, h, span), bf16),
            pltpu.VMEM((pieces, tp_n - 1, h, span), bf16),
            pltpu.VMEM((CHUNKS, tp_n, h, 128), f32),
            pltpu.VMEM((CHUNKS, tp_n, h, 128), f32),
            pltpu.VMEM((CHUNKS, 8, tp_n * h), f32),
            pltpu.VMEM((CHUNKS, tp_n, 8, tp_n * h), f32),
            pltpu.VMEM((CHUNKS, tp_n, h, width), f32),
            pltpu.VMEM((CHUNKS, tp_n, h, 128), f32),
            pltpu.VMEM((CHUNKS, g_n, q, h, width), bf16),
            pltpu.VMEM((CHUNKS, g_n, q, h, width), bf16),
            dma((tp_n,)), dma((PARTS,)), dma((DEC_BLOCKS,)),
            dma((CHUNKS, n_stage)), dma((CHUNKS, n_stage)),
            dma((CHUNKS, g_n)), dma((CHUNKS, g_n)),
            dma((g_n,)), dma((g_n,)),
            dma((pieces, n_stage)), dma((pieces, n_stage)),
            dma((CHUNKS, tp_n)), dma((CHUNKS, tp_n)),
            dma((CHUNKS, g_n)), dma((CHUNKS, g_n)),
        ],
        compiler_params=pltpu.CompilerParams(
            collective_id=0, has_side_effects=True, vmem_limit_bytes=60 * 2**20
        ),
    )(
        ho.reshape(q, CHUNKS, h, depth),
        resid_in.reshape(q, CHUNKS, h, width),
        table.reshape(q, CHUNKS, h, 128),
        enc_bias.reshape(1, lat),
        out_weight, enc_weight, dec_weight,
    )
    return resid_out.reshape(rc, width), feat


def per_device(
    resid_in,
    queries,
    kv_cache,
    new_kv,
    lengths,
    out_weight,
    enc_weight,
    enc_bias,
    dec_weight,
    clamp_ids,
    clamp_values,
):
    tp_count = lax.axis_size("tp")
    tp_rank = lax.axis_index("tp")
    row_count = resid_in.shape[0]
    own_heads = queries.shape[1] // HEAD_DIM
    slot_count = kv_cache.shape[3]
    score_scale = HEAD_DIM ** (-0.5)
    query_heads = queries.reshape(row_count, own_heads, HEAD_DIM)
    cache_keys = kv_cache[0, :, 0]
    cache_values = kv_cache[1, :, 0]
    kv_index = tp_rank // (tp_count // KV_HEADS)
    new_key = lax.dynamic_index_in_dim(new_kv[0], kv_index, 1, keepdims=False)
    new_value = lax.dynamic_index_in_dim(new_kv[1], kv_index, 1, keepdims=False)
    scores = (
        jnp.einsum("shd,spd->shp", query_heads, cache_keys, preferred_element_type=jnp.float32)
        * score_scale
    )
    new_score = (
        jnp.einsum("shd,sd->sh", query_heads, new_key, preferred_element_type=jnp.float32)
        * score_scale
    )
    slot_index = jnp.arange(slot_count, dtype=jnp.int32)
    is_valid = (slot_index[None, :] < lengths[:, None])[:, None, :]
    top_score = jnp.maximum(jnp.max(jnp.where(is_valid, scores, -jnp.inf), axis=-1), new_score)
    prob_cache = jnp.where(is_valid, jnp.exp(scores - top_score[..., None]), 0.0)
    new_prob = jnp.exp(new_score - top_score)
    total_weight = jnp.sum(prob_cache, axis=-1) + new_prob
    new_rounded = lax.optimization_barrier(new_prob.astype(jnp.bfloat16)).astype(jnp.float32)
    weighted = jnp.einsum(
        "shp,spd->shd",
        prob_cache.astype(jnp.bfloat16),
        cache_values,
        preferred_element_type=jnp.float32,
    )
    weighted = weighted + new_rounded[..., None] * new_value.astype(jnp.float32)[:, None, :]
    head_output = (
        (weighted / total_weight[..., None])
        .astype(jnp.bfloat16)
        .reshape(row_count, own_heads * HEAD_DIM)
    )
    slots = clamp_ids.shape[1]
    table = jnp.concatenate(
        [
            clamp_ids.astype(jnp.float32),
            clamp_values,
            jnp.zeros((row_count, 128 - 2 * slots), jnp.float32),
        ],
        axis=1,
    )
    resid_out, feature_out = layer(
        head_output, resid_in, table, enc_bias, out_weight, enc_weight, dec_weight, slots
    )
    return (resid_out, feature_out)


def solution(mesh):
    placed = (
        P("grp", "tp"),
        P("grp", "tp"),
        P(None, "grp", "tp", None, None),
        P(None, "grp", None, None),
        P("grp"),
        P("tp", None),
        P("tp", "grp"),
        P("grp"),
        P("grp", "tp"),
        P("grp", None),
        P("grp", None),
    )
    return jax.shard_map(
        per_device,
        mesh=mesh,
        in_specs=placed,
        out_specs=(P("grp", "tp"), P("tp", "grp")),
        check_vma=False,
    )
```

```python
import functools

import jax
import jax.numpy as jnp
from jax import lax
from jax.experimental import pallas as pl
from jax.experimental.pallas import tpu as pltpu
from jax.sharding import PartitionSpec as P

HEAD_DIM = 128
KV_HEADS = 4
CHUNKS = 2
PARTS = 4
DEC_BLOCKS = 8
DEC_SLOTS = 4
TILE = 256
MESH = pl.DeviceIdType.MESH


def bits_of(count):
    found, bit = [], 1
    while bit < count:
        found.append(bit)
        bit *= 2
    return found


def flip(rank, pattern, count):
    for bit in bits_of(count):
        if pattern & bit:
            rank = rank + bit * (1 - 2 * lax.rem(lax.div(rank, bit), 2))
    return rank


def stage_plan(count, ascending):
    order = bits_of(count)
    order = order if ascending else order[:1] + order[:0:-1]
    held, stages = list(range(count)), []
    for bit in order:
        keep = [i for i, e in enumerate(held) if not e & bit]
        send = [held.index(held[i] + bit) for i in keep]
        stages.append((bit, keep, send))
        held = [held[i] for i in keep]
    return stages


def layer_kernel(
    cfg,
    ho_ref, resid_ref, table_ref, bias_ref, outw_ref, enc_ref, dec_ref,
    resid_out_ref, feat_ref,
    ho_p, outw_v, enc_v, dec_v,
    a_keep, a_send, a_recv,
    xg, xp, tg, lid_d, lid_e,
    p_keep, p_send, p_recv,
    acc, picked, pk_send, pk_recv, rows, delta, e_send, e_recv,
    outw_sem, enc_sem, dec_sem,
    a_ss, a_rs, x_ss, x_rs, t_ss, t_rs, p_ss, p_rs, k_ss, k_rs, e_ss, e_rs,
):
    tp_n, g_n, slots = cfg
    t, g = lax.axis_index("tp"), lax.axis_index("grp")
    q, _, h, width = resid_ref.shape
    lat = bias_ref.shape[1]
    span = lat // PARTS
    half = q * h
    rows_m = tp_n * h
    block = lat // DEC_BLOCKS
    own = pl.ds(g * q, q)
    tile = min(TILE, span)

    def remote(src, dst, ss, rs, axis, other):
        return pltpu.make_async_remote_copy(
            src_ref=src, dst_ref=dst, send_sem=ss, recv_sem=rs,
            device_id={axis: other}, device_id_type=MESH,
        )

    order_e = [e for e in range(tp_n) if e & 1] + [e for e in range(tp_n) if not e & 1]

    def outw_copy(e):
        cols = pl.ds(pl.multiple_of(flip(t, e, tp_n) * width, width), width)
        return pltpu.make_async_copy(outw_ref.at[:, cols], outw_v.at[e], outw_sem.at[e])

    def enc_copy(c):
        return pltpu.make_async_copy(
            enc_ref.at[:, pl.ds(c * span, span)], enc_v.at[c], enc_sem.at[c]
        )

    def dec_copy(b):
        return pltpu.make_async_copy(
            dec_ref.at[pl.ds(b * block, block)], dec_v.at[b % DEC_SLOTS], dec_sem.at[b]
        )

    for e in order_e:
        outw_copy(e).start()

    barrier = pltpu.get_barrier_semaphore()
    for e in range(1, tp_n):
        pl.semaphore_signal(
            barrier, inc=1, device_id={"tp": flip(t, e, tp_n)}, device_id_type=MESH
        )
    for e in range(1, g_n):
        pl.semaphore_signal(
            barrier, inc=1, device_id={"grp": flip(g, e, g_n)}, device_id_type=MESH
        )
    for j in range(CHUNKS):
        ho_p[j] = ho_ref[:, j].reshape(half, ho_ref.shape[3])
    tg[own] = table_ref[...]
    pl.semaphore_wait(barrier, tp_n + g_n - 2)

    table_copies = []
    for e in range(1, g_n):
        copy = remote(
            table_ref, tg.at[own], t_ss.at[e], t_rs.at[e], "grp", flip(g, e, g_n)
        )
        copy.start()
        table_copies.append(copy)

    plans = [stage_plan(tp_n, True), stage_plan(tp_n, False)]
    n_stage = len(plans[0])

    def a_copy(j, k):
        bit = plans[j % 2][k][0]
        count = tp_n >> (k + 1)
        first = tp_n - 2 * count
        part = pl.ds(first, count)
        return remote(
            a_send.at[j, part], a_recv.at[j, part], a_ss.at[j, k], a_rs.at[j, k],
            "tp", flip(t, bit, tp_n),
        )

    for place, e in enumerate(order_e):
        outw_copy(e).wait()
        part = jnp.dot(
            ho_p[...].reshape(CHUNKS * half, ho_p.shape[2]), outw_v[e],
            preferred_element_type=jnp.float32,
        )
        for j in range(CHUNKS):
            mine = part[j * half : (j + 1) * half]
            if e & 1:
                a_send[j, e >> 1] = mine.astype(jnp.bfloat16)
            else:
                a_keep[j, e >> 1] = mine
        if place == tp_n // 2 - 1:
            for j in range(CHUNKS):
                a_copy(j, 0).start()
    for c in range(PARTS):
        enc_copy(c).start()
    for b in range(DEC_SLOTS):
        dec_copy(b).start()

    def held_at(plan, k):
        held = list(range(tp_n // 2))
        for _, stay, _ in plan[1 : k + 1]:
            held = [held[s] for s in stay]
        return held

    def fold(keep, send, recv, copy, plan, j, k):
        copy(j, k - 1).wait()
        count = tp_n >> k
        first = tp_n - 2 * count
        held = held_at(plan, k - 1)
        for i, slot in enumerate(held):
            keep[j, slot] = keep[j, slot] + recv[j, first + i].astype(jnp.float32)
        if k < n_stage:
            go = plan[k][2]
            nxt = tp_n - 2 * (count // 2)
            for i, s in enumerate(go):
                send[j, nxt + i] = keep[j, held[s]].astype(jnp.bfloat16)
            copy(j, k).start()

    for k in range(1, n_stage + 1):
        for j in range(CHUNKS):
            fold(a_keep, a_send, a_recv, a_copy, plans[j % 2], j, k)

    x_copies = [[], []]
    for j in range(CHUNKS):
        mid = resid_ref[:, j].astype(jnp.float32) + a_keep[j, 0].reshape(q, h, width)
        xg[j, own] = mid.astype(jnp.bfloat16)
        for e in range(1, g_n):
            copy = remote(
                xg.at[j, own], xg.at[j, own], x_ss.at[j, e], x_rs.at[j, e],
                "grp", flip(g, e, g_n),
            )
            copy.start()
            x_copies[j].append(copy)

    for copy in table_copies:
        copy.wait()
    low = (g * lat).astype(jnp.float32)
    for j in range(CHUNKS):
        found = tg[:, j].reshape(rows_m, 128)
        local = jnp.full((rows_m, 1), -1.0, jnp.float32)
        value = jnp.zeros((rows_m, 1), jnp.float32)
        for c in range(slots):
            place = found[:, c : c + 1] - low
            inside = (place >= 0.0) & (place < float(lat))
            local = jnp.where(inside, place, local)
            value = jnp.where(inside, found[:, slots + c : slots + c + 1], value)
        wide = jnp.broadcast_to(local, (rows_m, 128)).astype(jnp.int32)
        lid_d[j] = wide.reshape(tp_n, h, 128)
        delta[j] = jnp.broadcast_to(value, (rows_m, 128)).reshape(tp_n, h, 128)
    for j in range(CHUNKS):
        for e in range(tp_n):
            lid_e[j, e] = lid_d[j, flip(t, e, tp_n)]
    acc[...] = jnp.zeros_like(acc)
    rows[...] = jnp.zeros_like(rows)

    def dec_step(b):
        dec_copy(b).wait()
        lane = lax.broadcasted_iota(jnp.int32, (CHUNKS * rows_m, 128), 1)
        local = lid_d[...].reshape(CHUNKS * rows_m, 128)
        pieces = [
            jnp.where(local == lane + (b * block + n), 1.0, 0.0).astype(jnp.bfloat16)
            for n in range(0, block, 128)
        ]
        hot = jnp.concatenate(pieces, axis=1)
        got = jnp.dot(hot, dec_v[b % DEC_SLOTS], preferred_element_type=jnp.float32)
        rows[...] += got.reshape(rows.shape)
        if b + DEC_SLOTS < DEC_BLOCKS:
            dec_copy(b + DEC_SLOTS).start()

    for b in range(DEC_SLOTS):
        dec_step(b)

    pieces = CHUNKS * PARTS
    bias_on = jnp.where(t == 0, 1.0, 0.0).astype(jnp.float32)

    def p_copy(p, k):
        bit = plans[p % 2][k][0]
        count = tp_n >> (k + 1)
        part = pl.ds(tp_n - 2 * count, count)
        return remote(
            p_send.at[p, part], p_recv.at[p, part], p_ss.at[p, k], p_rs.at[p, k],
            "tp", flip(t, bit, tp_n),
        )

    def multiply(p):
        j, c = p // PARTS, p % PARTS
        if c == 0:
            for copy in x_copies[j]:
                copy.wait()
            for e in range(tp_n):
                xp[j, e] = xg[j, flip(t, e, tp_n)]
        if j == 0:
            enc_copy(c).wait()

        def body(n, _):
            cols = pl.ds(pl.multiple_of(n * tile, tile), tile)
            part = jnp.dot(
                xp[j].reshape(rows_m, width), enc_v[c, :, cols],
                preferred_element_type=jnp.float32,
            )
            lane = lax.broadcasted_iota(jnp.int32, (rows_m, 128), 1)
            local = lid_e[j].reshape(rows_m, 128)
            total = acc[j].reshape(rows_m, 128)
            for m in range(0, tile, 128):
                at = pl.multiple_of(c * span + n * tile + m, 128)
                shift = bias_ref[:, pl.ds(at, 128)] * bias_on
                total = total + jnp.where(
                    local == lane + at, part[:, m : m + 128] + shift, 0.0
                )
            acc[j] = total.reshape(tp_n, h, 128)
            for e in range(tp_n):
                rows_e = part[e * h : (e + 1) * h]
                if e & 1:
                    p_send[p, e >> 1, :, cols] = rows_e.astype(jnp.bfloat16)
                else:
                    p_keep[p, e >> 1, :, cols] = rows_e
            return 0

        lax.fori_loop(0, span // tile, body, 0)
        p_copy(p, 0).start()

    def finish(p):
        j, c = p // PARTS, p % PARTS
        cols = pl.ds(c * span, span)
        whole = p_keep[p, 0] + bias_ref[:, cols]
        feat_ref[pl.ds(j * h, h), cols] = jnp.maximum(whole, 0.0).astype(jnp.bfloat16)

    eye = lax.broadcasted_iota(jnp.int32, (rows_m, rows_m), 0) == lax.broadcasted_iota(
        jnp.int32, (rows_m, rows_m), 1
    )

    def pick_copy(j, e):
        return remote(
            pk_send.at[j], pk_recv.at[j, e], k_ss.at[j, e], k_rs.at[j, e],
            "tp", flip(t, e, tp_n),
        )

    def pick(j):
        for e in range(tp_n):
            picked[j, flip(t, e, tp_n)] = acc[j, e]
        column = jnp.sum(picked[j].reshape(rows_m, 128), axis=1, keepdims=True)
        line = jnp.sum(jnp.where(eye, column, 0.0), axis=0, keepdims=True)
        pk_send[j] = jnp.broadcast_to(line, (8, rows_m))
        for e in range(1, tp_n):
            pick_copy(j, e).start()

    def edit_copy(j, e):
        return remote(
            e_send.at[j, e], e_recv.at[j, e], e_ss.at[j, e], e_rs.at[j, e],
            "grp", flip(g, e, g_n),
        )

    def edit(j):
        line = pk_send[j]
        for e in range(1, tp_n):
            pick_copy(j, e).wait()
            line = line + pk_recv[j, e]
        column = jnp.sum(jnp.where(eye, line[:1], 0.0), axis=1, keepdims=True)
        now = jnp.maximum(column, 0.0).astype(jnp.bfloat16).astype(jnp.float32)
        change = delta[j].reshape(rows_m, 128)[:, :1] - now
        change = change.astype(jnp.bfloat16).astype(jnp.float32)
        delta[j] = jnp.broadcast_to(change, (rows_m, 128)).reshape(tp_n, h, 128)
        for e in range(1, g_n):
            there = pl.ds(flip(g, e, g_n) * q, q)
            step = delta[j, there]
            e_send[j, e] = (rows[j, there] * step[:, :, :1]).astype(jnp.bfloat16)
            edit_copy(j, e).start()

    def close(j):
        total = xg[j, own].astype(jnp.float32)
        edits = rows[j, own] * delta[j, own][:, :, :1]
        for e in range(1, g_n):
            edit_copy(j, e).wait()
            edits = edits + e_recv[j, e].astype(jnp.float32)
        resid_out_ref[:, j] = (total + edits).astype(jnp.bfloat16)

    for s in range(pieces + 2 * n_stage - 1):
        if s < pieces:
            multiply(s)
            if s % PARTS == PARTS - 1:
                pick(s // PARTS)
        for k in range(1, n_stage + 1):
            p = s - 2 * k + 1
            if 0 <= p < pieces:
                fold(p_keep, p_send, p_recv, p_copy, plans[p % 2], p, k)
                if k == n_stage:
                    finish(p)
            if k == 1 and s == PARTS:
                edit(0)
            if k == 1 and s == pieces:
                edit(1)
        if s < DEC_BLOCKS - DEC_SLOTS:
            dec_step(s + DEC_SLOTS)
    for j in range(CHUNKS):
        close(j)


def layer(ho, resid_in, table, enc_bias, out_weight, enc_weight, dec_weight, slots):
    tp_n, g_n = lax.axis_size("tp"), lax.axis_size("grp")
    rc, width = resid_in.shape
    depth = ho.shape[1]
    lat = enc_weight.shape[1]
    out_rows = rc * g_n // tp_n
    q, h = rc // out_rows, out_rows // CHUNKS
    half = q * h
    span, block = lat // PARTS, lat // DEC_BLOCKS
    pieces = CHUNKS * PARTS
    n_stage = len(bits_of(tp_n))
    bf16, f32 = jnp.bfloat16, jnp.float32
    vmem = pl.BlockSpec(memory_space=pltpu.VMEM)
    hbm = pl.BlockSpec(memory_space=pl.ANY)
    dma = pltpu.SemaphoreType.DMA
    resid_out, feat = pl.pallas_call(
        functools.partial(layer_kernel, (tp_n, g_n, slots)),
        out_shape=(
            jax.ShapeDtypeStruct((q, CHUNKS, h, width), bf16),
            jax.ShapeDtypeStruct((out_rows, lat), bf16),
        ),
        in_specs=[vmem, vmem, vmem, vmem, hbm, hbm, hbm],
        out_specs=(vmem, vmem),
        scratch_shapes=[
            pltpu.VMEM((CHUNKS, half, depth), bf16),
            pltpu.VMEM((tp_n, depth, width), bf16),
            pltpu.VMEM((PARTS, width, span), bf16),
            pltpu.VMEM((DEC_SLOTS, block, width), bf16),
            pltpu.VMEM((CHUNKS, tp_n // 2, half, width), f32),
            pltpu.VMEM((CHUNKS, tp_n - 1, half, width), bf16),
            pltpu.VMEM((CHUNKS, tp_n - 1, half, width), bf16),
            pltpu.VMEM((CHUNKS, tp_n, h, width), bf16),
            pltpu.VMEM((CHUNKS, tp_n, h, width), bf16),
            pltpu.VMEM((tp_n, CHUNKS, h, 128), f32),
            pltpu.VMEM((CHUNKS, tp_n, h, 128), jnp.int32),
            pltpu.VMEM((CHUNKS, tp_n, h, 128), jnp.int32),
            pltpu.VMEM((pieces, tp_n // 2, h, span), f32),
            pltpu.VMEM((pieces, tp_n - 1, h, span), bf16),
            pltpu.VMEM((pieces, tp_n - 1, h, span), bf16),
            pltpu.VMEM((CHUNKS, tp_n, h, 128), f32),
            pltpu.VMEM((CHUNKS, tp_n, h, 128), f32),
            pltpu.VMEM((CHUNKS, 8, tp_n * h), f32),
            pltpu.VMEM((CHUNKS, tp_n, 8, tp_n * h), f32),
            pltpu.VMEM((CHUNKS, tp_n, h, width), f32),
            pltpu.VMEM((CHUNKS, tp_n, h, 128), f32),
            pltpu.VMEM((CHUNKS, g_n, q, h, width), bf16),
            pltpu.VMEM((CHUNKS, g_n, q, h, width), bf16),
            dma((tp_n,)), dma((PARTS,)), dma((DEC_BLOCKS,)),
            dma((CHUNKS, n_stage)), dma((CHUNKS, n_stage)),
            dma((CHUNKS, g_n)), dma((CHUNKS, g_n)),
            dma((g_n,)), dma((g_n,)),
            dma((pieces, n_stage)), dma((pieces, n_stage)),
            dma((CHUNKS, tp_n)), dma((CHUNKS, tp_n)),
            dma((CHUNKS, g_n)), dma((CHUNKS, g_n)),
        ],
        compiler_params=pltpu.CompilerParams(
            collective_id=0, has_side_effects=True, vmem_limit_bytes=60 * 2**20
        ),
    )(
        ho.reshape(q, CHUNKS, h, depth),
        resid_in.reshape(q, CHUNKS, h, width),
        table.reshape(q, CHUNKS, h, 128),
        enc_bias.reshape(1, lat),
        out_weight, enc_weight, dec_weight,
    )
    return resid_out.reshape(rc, width), feat


def per_device(
    resid_in,
    queries,
    kv_cache,
    new_kv,
    lengths,
    out_weight,
    enc_weight,
    enc_bias,
    dec_weight,
    clamp_ids,
    clamp_values,
):
    tp_count = lax.axis_size("tp")
    tp_rank = lax.axis_index("tp")
    row_count = resid_in.shape[0]
    own_heads = queries.shape[1] // HEAD_DIM
    slot_count = kv_cache.shape[3]
    score_scale = HEAD_DIM ** (-0.5)
    query_heads = queries.reshape(row_count, own_heads, HEAD_DIM)
    cache_keys = kv_cache[0, :, 0]
    cache_values = kv_cache[1, :, 0]
    kv_index = tp_rank // (tp_count // KV_HEADS)
    new_key = lax.dynamic_index_in_dim(new_kv[0], kv_index, 1, keepdims=False)
    new_value = lax.dynamic_index_in_dim(new_kv[1], kv_index, 1, keepdims=False)
    scores = (
        jnp.einsum("shd,spd->shp", query_heads, cache_keys, preferred_element_type=jnp.float32)
        * score_scale
    )
    new_score = (
        jnp.einsum("shd,sd->sh", query_heads, new_key, preferred_element_type=jnp.float32)
        * score_scale
    )
    slot_index = jnp.arange(slot_count, dtype=jnp.int32)
    is_valid = (slot_index[None, :] < lengths[:, None])[:, None, :]
    top_score = jnp.maximum(jnp.max(jnp.where(is_valid, scores, -jnp.inf), axis=-1), new_score)
    prob_cache = jnp.where(is_valid, jnp.exp(scores - top_score[..., None]), 0.0)
    new_prob = jnp.exp(new_score - top_score)
    total_weight = jnp.sum(prob_cache, axis=-1) + new_prob
    new_rounded = lax.optimization_barrier(new_prob.astype(jnp.bfloat16)).astype(jnp.float32)
    weighted = jnp.einsum(
        "shp,spd->shd",
        prob_cache.astype(jnp.bfloat16),
        cache_values,
        preferred_element_type=jnp.float32,
    )
    weighted = weighted + new_rounded[..., None] * new_value.astype(jnp.float32)[:, None, :]
    head_output = (
        (weighted / total_weight[..., None])
        .astype(jnp.bfloat16)
        .reshape(row_count, own_heads * HEAD_DIM)
    )
    slots = clamp_ids.shape[1]
    table = jnp.concatenate(
        [
            clamp_ids.astype(jnp.float32),
            clamp_values,
            jnp.zeros((row_count, 128 - 2 * slots), jnp.float32),
        ],
        axis=1,
    )
    resid_out, feature_out = layer(
        head_output, resid_in, table, enc_bias, out_weight, enc_weight, dec_weight, slots
    )
    return (resid_out, feature_out)


def solution(mesh):
    placed = (
        P("grp", "tp"),
        P("grp", "tp"),
        P(None, "grp", "tp", None, None),
        P(None, "grp", None, None),
        P("grp"),
        P("tp", None),
        P("tp", "grp"),
        P("grp"),
        P("grp", "tp"),
        P("grp", None),
        P("grp", None),
    )
    return jax.shard_map(
        per_device,
        mesh=mesh,
        in_specs=placed,
        out_specs=(P("grp", "tp"), P("tp", "grp")),
        check_vma=False,
    )
```
